32 devices in a mesh: ctx: 8 (over z, y), head: 4 (over x, core).
Axes of the slice: x: 2, y: 2, z: 4, core: 2. Of those that a mesh axis runs over, the one named last changes fastest.
Arguments:
- queries: bfloat16 [2048, 6144], P(('ctx', 'head')), may hold values from -120 to 120
- keys: bfloat16 [2048, 1024], P(('ctx', 'head')), may hold values from -6 to 6
- values: bfloat16 [2048, 1024], P(('ctx', 'head')), may hold values from -6 to 6
- outputs: bfloat16 [2048, 6144], P(('ctx', 'head')), may hold values from -6 to 6
- out_grad: bfloat16 [2048, 6144], P(('ctx', 'head')), may hold values from -6 to 6
- frame_lists: int32 [8, 5], P('ctx'), may hold values from -1 to 7, as said below
Outputs:
- grad_queries: bfloat16 [2048, 6144], P('ctx', 'head')
- key_gradient: bfloat16 [2048, 1024], P('ctx', 'head')
- value_gradient: bfloat16 [2048, 1024], P('ctx', 'head')
The draws below stay inside these ranges and needn't reach their ends.
Inputs may be any that keep to these rules, and one draw needn't show every extreme that they name: `frame_lists`: entry o of the list of query frame f is f - o or -1 (always -1 where f - o < 0); entry 0 is f; entry 4 is f - 4 for every frame f divisible by 3 with f >= 4.
All inputs are finite; a program needn't handle non-finite values.
Results may differ from the reference program's by a relative error of at most 0.005.
Values may be sent and summed in bfloat16 or wider, within the bound.
A program may use at most 64 MiB of HBM per device.

```python
import jax
import jax.numpy as jnp
from jax import lax

QUERY_HEAD_COUNT = 48
KEY_VALUE_HEADS = 8
HEAD_SIZE = 128
TOK_DEV = 256
FRAME = 256
REACH = 4
SEQUENCE_TOKENS = 2048
FRAMES = 8
LIST = 5
N_CTX = 8


def attention_pair(key):
    base = jax.random.fold_in(key, 11)
    key_query, key_random_seed = jax.random.split(base, 2)
    query_draw = jnp.clip(jax.random.normal(key_query, (SEQUENCE_TOKENS, QUERY_HEAD_COUNT * HEAD_SIZE), jnp.float32), -6.0, 6.0)
    key_sample = jnp.clip(jax.random.normal(key_random_seed, (SEQUENCE_TOKENS, KEY_VALUE_HEADS * HEAD_SIZE), jnp.float32), -6.0, 6.0)
    return (query_draw, key_sample)


def draw_queries(key, part):
    return attention_pair(key)[0].astype(jnp.bfloat16)


def draw_keys(key, part):
    return attention_pair(key)[1].astype(jnp.bfloat16)


def draw_frame_lists(key, part):
    frame_pos = jnp.arange(FRAMES, dtype=jnp.int32)[:, None]
    offset = jnp.arange(LIST, dtype=jnp.int32)[None, :]
    coin = jax.random.randint(jax.random.fold_in(key, 23), (FRAMES, LIST), 0, 2)
    keep = (coin == 1) | (offset == 0) | (offset == LIST - 1) & (frame_pos % 3 == 0)
    return jnp.where(keep & (frame_pos - offset >= 0), frame_pos - offset, -1).astype(jnp.int32)


def steps_of(rng, dims, pieces, low, high):
    loudness = 1.0
    for position, blocks in pieces:
        heights = jax.random.uniform(jax.random.fold_in(jax.random.fold_in(rng, 6), position), (blocks,), jnp.float32, low / len(pieces), high / len(pieces))
        loudness = loudness * jnp.repeat(jnp.exp(heights), dims[position] // blocks).reshape((-1,) + (1,) * (len(dims) - 1 - position))
    return loudness


def noise(stream_key, extent, spread, most, shards=(), held_as=jnp.bfloat16):
    entries = jax.random.normal(stream_key, extent, jnp.float32) * spread
    if len(shards) > 0:
        entries = steps_of(stream_key, extent, shards, -0.22, 0.18) * entries
    return jnp.clip(entries, min=-most, max=most).astype(held_as)


def setup_inputs(seed: int = 0) -> dict:
    key_of = jax.random.split(jax.random.key(seed), 7)
    return {
        "queries": draw_queries(jax.random.fold_in(key_of[6], 71), 0),
        "keys": draw_keys(jax.random.fold_in(key_of[6], 71), 0),
        "values": noise(key_of[2], (SEQUENCE_TOKENS, KEY_VALUE_HEADS * HEAD_SIZE), 1.0, 6.0, ((0, 32),)),
        "outputs": noise(key_of[3], (SEQUENCE_TOKENS, QUERY_HEAD_COUNT * HEAD_SIZE), 1.0, 6.0, ((0, 32),)),
        "out_grad": noise(key_of[4], (SEQUENCE_TOKENS, QUERY_HEAD_COUNT * HEAD_SIZE), 1.0, 6.0, ((0, 32),)),
        "frame_lists": draw_frame_lists(jax.random.fold_in(key_of[6], 71), 0),
    }


def reference(queries, keys, values, outputs, out_grad, frame_lists):
    score_scaling = HEAD_SIZE ** -0.5
    frame_window = REACH * TOK_DEV
    query_group_width = QUERY_HEAD_COUNT // KEY_VALUE_HEADS
    frames_dev = TOK_DEV // FRAME
    key_extent = frame_window + TOK_DEV
    key_padding = jnp.concatenate([jnp.zeros((frame_window, KEY_VALUE_HEADS * HEAD_SIZE), keys.dtype), keys], axis=0)
    value_padding = jnp.concatenate([jnp.zeros((frame_window, KEY_VALUE_HEADS * HEAD_SIZE), values.dtype), values], axis=0)
    row_delta = jnp.sum((out_grad.astype(jnp.float32) * outputs.astype(jnp.float32)).reshape(SEQUENCE_TOKENS, QUERY_HEAD_COUNT, HEAD_SIZE), axis=2)

    def block(carry, block_index):
        key_gradient, value_gradient = carry
        start_position = (block_index * TOK_DEV).astype(jnp.int32)
        query_block_rows = lax.dynamic_slice_in_dim(queries, start_position, TOK_DEV, 0).reshape(TOK_DEV, QUERY_HEAD_COUNT, HEAD_SIZE).astype(jnp.float32)
        gradient_block = lax.dynamic_slice_in_dim(out_grad, start_position, TOK_DEV, 0).reshape(TOK_DEV, QUERY_HEAD_COUNT, HEAD_SIZE).astype(jnp.float32)
        delta_blk = lax.dynamic_slice_in_dim(row_delta, start_position, TOK_DEV, 0)
        key_block_rows = lax.dynamic_slice_in_dim(key_padding, start_position, key_extent, 0).reshape(key_extent, KEY_VALUE_HEADS, HEAD_SIZE).astype(jnp.float32)
        value_block_rows = lax.dynamic_slice_in_dim(value_padding, start_position, key_extent, 0).reshape(key_extent, KEY_VALUE_HEADS, HEAD_SIZE).astype(jnp.float32)
        key_wide = jnp.repeat(key_block_rows, query_group_width, axis=1)
        value_wide = jnp.repeat(value_block_rows, query_group_width, axis=1)
        lists = lax.dynamic_slice_in_dim(frame_lists, (block_index * frames_dev).astype(jnp.int32), frames_dev, 0)
        key_tok = start_position - frame_window + jnp.arange(key_extent, dtype=jnp.int32)
        key_frame = jnp.floor_divide(key_tok, FRAME)
        listed = jnp.any(lists[:, :, None] == key_frame[None, None, :], axis=1) & (key_tok >= 0)[None, :]
        allowed = jnp.repeat(listed, FRAME, axis=0)
        scores = jnp.einsum('thd,lhd->htl', query_block_rows, key_wide) * score_scaling
        scores = jnp.where(allowed[None], scores, -jnp.inf)
        peak = jnp.max(scores, axis=2, keepdims=True)
        lse = peak + jnp.log(jnp.sum(jnp.exp(scores - peak), axis=2, keepdims=True))
        probs = jnp.exp(scores - lse)
        probability_block = lax.optimization_barrier(probs.astype(jnp.bfloat16)).astype(jnp.float32)
        dprobs = jnp.einsum('thd,lhd->htl', gradient_block, value_wide)
        dscores = probs * (dprobs - delta_blk.T[:, :, None])
        score_gradient_block = lax.optimization_barrier(dscores.astype(jnp.bfloat16)).astype(jnp.float32)
        grad_q = (jnp.einsum('htl,lhd->thd', score_gradient_block, key_wide) * score_scaling).astype(jnp.bfloat16)
        key_gradient_terms = jnp.einsum('yzk,zyq->kyq', score_gradient_block, query_block_rows).reshape(key_extent, KEY_VALUE_HEADS, query_group_width, HEAD_SIZE).sum(axis=2) * score_scaling
        value_gradient_terms = jnp.einsum('yzk,zyq->kyq', probability_block, gradient_block).reshape(key_extent, KEY_VALUE_HEADS, query_group_width, HEAD_SIZE).sum(axis=2)
        earlier_keys = lax.dynamic_slice_in_dim(key_gradient, start_position, key_extent, 0)
        earlier_values = lax.dynamic_slice_in_dim(value_gradient, start_position, key_extent, 0)
        key_gradient = lax.dynamic_update_slice_in_dim(key_gradient, earlier_keys + key_gradient_terms.reshape(key_extent, KEY_VALUE_HEADS * HEAD_SIZE), start_position, 0)
        value_gradient = lax.dynamic_update_slice_in_dim(value_gradient, earlier_values + value_gradient_terms.reshape(key_extent, KEY_VALUE_HEADS * HEAD_SIZE), start_position, 0)
        return (key_gradient, value_gradient), grad_q.reshape(TOK_DEV, QUERY_HEAD_COUNT * HEAD_SIZE)

    empty_block = jnp.zeros((frame_window + SEQUENCE_TOKENS, KEY_VALUE_HEADS * HEAD_SIZE), jnp.float32)
    (key_gradient, value_gradient), grad_blocks = lax.scan(block, (empty_block, empty_block), jnp.arange(N_CTX, dtype=jnp.int32))
    grad_queries = grad_blocks.reshape(SEQUENCE_TOKENS, QUERY_HEAD_COUNT * HEAD_SIZE)
    return grad_queries, key_gradient[frame_window:].astype(jnp.bfloat16), value_gradient[frame_window:].astype(jnp.bfloat16)
```

```python
import functools

import jax
import jax.numpy as jnp
from jax import lax
from jax.experimental import pallas as pl
from jax.experimental.pallas import tpu as pltpu
from jax.sharding import PartitionSpec as P

MESH = pl.DeviceIdType.MESH
HEAD_SIZE = 128
FRAME = 256
REACH = 4
BLOCKS = REACH + 1
LOG2E = 1.4426950408889634
LAST = (((1,), (1,)), ((), ()))


def dot(a, b):
    return jnp.dot(a, b, preferred_element_type=jnp.float32)


def dot_last(a, b):
    return lax.dot_general(a, b, LAST, preferred_element_type=jnp.float32)


def kernel(
    n_ctx, n_head, kv_count, width,
    q_ref, k_ref, v_ref, o_ref, g_ref, list_ref,
    dq_ref, dk_ref, dv_ref,
    qb, gb, kvb, kt, g_loc, o_loc, d_out, d_in, delta, sc, acc, out_buf, in_buf,
    own_sem, in_sem, a_send, a_recv, d_send, d_recv, f_send, f_recv, r_send, r_recv,
):
    c = lax.axis_index("ctx")
    h = lax.axis_index("head")
    y = lax.rem(c, 2)
    across = c + 1 - 2 * y
    rows = q_ref.shape[0]
    tokens = rows * n_head
    heads = kv_count * width
    scale = HEAD_SIZE ** -0.5

    g_in = pltpu.make_async_copy(g_ref, g_loc, in_sem.at[0])
    o_in = pltpu.make_async_copy(o_ref, o_loc, in_sem.at[1])
    g_in.start()
    o_in.start()

    barrier = pltpu.get_barrier_semaphore()
    peers = [lax.rem(h + r, n_head) for r in range(1, n_head)]
    for p in peers:
        pl.semaphore_signal(barrier, inc=1, device_id=(c, p), device_id_type=MESH)
    pl.semaphore_signal(barrier, inc=1, device_id=(across, h), device_id_type=MESH)

    @pl.when(c + 2 < n_ctx)
    def _():
        pl.semaphore_signal(barrier, inc=1, device_id=(c + 2, h), device_id_type=MESH)

    @pl.when(c >= 2)
    def _():
        pl.semaphore_signal(barrier, inc=1, device_id=(c - 2, h), device_id_type=MESH)

    ends = jnp.where(c + 2 < n_ctx, 1, 0) + jnp.where(c >= 2, 1, 0)
    pl.semaphore_wait(barrier, n_head + ends)

    my_rows = pl.ds(pl.multiple_of(h * rows, rows), rows)

    def piece(what, j, p):
        if what < 2:
            start = pl.multiple_of((p * kv_count + j) * HEAD_SIZE, HEAD_SIZE)
            ref = (k_ref, v_ref)[what]
            return ref.at[:, pl.ds(start, HEAD_SIZE)], kvb.at[j, 0, what, my_rows, :]
        span = width * HEAD_SIZE
        start = pl.multiple_of((p * kv_count + j) * span, HEAD_SIZE)
        ref, place = ((q_ref, qb), (g_ref, gb))[what - 2]
        return ref.at[:, pl.ds(start, span)], place.at[j, my_rows, :]

    def remote(what, j, r):
        source, place = piece(what, j, peers[r])
        return pltpu.make_async_remote_copy(
            src_ref=source, dst_ref=place, send_sem=a_send.at[r, j, what], recv_sem=a_recv.at[r, j, what],
            device_id=(c, peers[r]), device_id_type=MESH,
        )

    def local(what, j):
        source, place = piece(what, j, h)
        return pltpu.make_async_copy(source, place, own_sem.at[j, what])

    def regroup(whats, j, do):
        for what in whats:
            for r in range(n_head - 1):
                do(remote(what, j, r))
            do(local(what, j))

    def start(copy):
        copy.start()

    def wait(copy):
        copy.wait()

    def forward(j, k):
        source, slot, target, holds = (
            (0, 2, c + 2, c + 2 < n_ctx),
            (2 * y, 1, across, c >= 2 * y),
            (2, 4, c + 2, (c + 2 < n_ctx) & (c >= 2)),
            (2 + 2 * y, 3, across, c >= 2 + 2 * y),
        )[k]
        copy = pltpu.make_async_remote_copy(
            src_ref=kvb.at[j, source], dst_ref=kvb.at[j, slot], send_sem=f_send.at[j, k],
            recv_sem=f_recv.at[j, k], device_id=(target, h), device_id_type=MESH,
        )
        return copy, holds

    def forward_start(j, k):
        copy, holds = forward(j, k)

        @pl.when(holds)
        def _():
            copy.start()

    def forward_sent(j, k):
        copy, holds = forward(j, k)

        @pl.when(holds)
        def _():
            copy.wait_send()

    def forward_here(j, k):
        copy, _ = forward(j, k)

        @pl.when(c >= (2, 1, 4, 3)[k])
        def _():
            copy.wait_recv()

    def spread(j):
        forward_start(j, 0)

        @pl.when(y == 0)
        def _():
            forward(j, 1)[0].start()
        forward_here(j, 0)
        forward_start(j, 2)

        @pl.when((y == 1) & (c >= 2))
        def _():
            forward(j, 1)[0].start()

        @pl.when((y == 0) & (c >= 2))
        def _():
            forward(j, 3)[0].start()
        forward_here(j, 2)

        @pl.when((y == 1) & (c >= 4))
        def _():
            forward(j, 3)[0].start()
        forward_here(j, 1)
        forward_here(j, 3)
        for k in range(4):
            forward_sent(j, k)

    def back(j, k):
        source, target, holds, comes = (
            (0, across, c >= 1, across >= 1),
            (1, across, c >= 3, across >= 3),
            (2, c - 2, c >= 4, (c >= 2) & (c + 2 < n_ctx)),
            (3, c - 2, c >= 2, c + 2 < n_ctx),
        )[k]
        copy = pltpu.make_async_remote_copy(
            src_ref=out_buf.at[j, source], dst_ref=in_buf.at[j, k], send_sem=r_send.at[j, k],
            recv_sem=r_recv.at[j, k], device_id=(target, h), device_id_type=MESH,
        )
        return copy, holds, comes

    def back_start(j, k, slot):
        copy, holds, _ = back(j, k)

        @pl.when(holds)
        def _():
            out_buf[j, k] = acc[j, slot].astype(jnp.bfloat16)
            copy.start()

    def back_add(j, k, slot):
        copy, _, comes = back(j, k)

        @pl.when(comes)
        def _():
            copy.wait_recv()
            acc[j, slot] += in_buf[j, k].astype(jnp.float32)

    def back_one(j):
        back_start(j, 1, 3)
        back_start(j, 0, 1)

    def back_two(j):
        back_add(j, 1, 2 + 2 * y)
        back_start(j, 2, 4)
        back_add(j, 0, 2 * y)

    def back_three(j):
        back_add(j, 2, 2)
        back_start(j, 3, 2)

    def back_four(j):
        back_add(j, 3, 0)
        cols = slice(j * HEAD_SIZE, (j + 1) * HEAD_SIZE)
        dk_ref[:, cols] = (acc[j, 0, 0] * scale).astype(jnp.bfloat16)
        dv_ref[:, cols] = acc[j, 0, 1].astype(jnp.bfloat16)
        for k in range(4):
            copy, holds, _ = back(j, k)

            @pl.when(holds)
            def _():
                copy.wait_send()

    regroup((0, 1), 0, start)
    regroup((2, 3), 0, start)
    for j in range(1, kv_count):
        regroup((0, 1), j, start)

    for o in range(1, BLOCKS):
        @pl.when(c < o)
        def _():
            kvb[:, o] = jnp.zeros((kv_count, 2, tokens, HEAD_SIZE), jnp.bfloat16)
    acc[...] = jnp.zeros(acc.shape, jnp.float32)
    d_out[...] = jnp.zeros(d_out.shape, jnp.float32)
    g_in.wait()
    o_in.wait()
    ones = jnp.ones((16, HEAD_SIZE), jnp.bfloat16)

    def delta_of(p, carry):
        for i in range(heads):
            cols = pl.ds(pl.multiple_of((p * heads + i) * HEAD_SIZE, HEAD_SIZE), HEAD_SIZE)
            product = g_loc[:, cols].astype(jnp.float32) * o_loc[:, cols].astype(jnp.float32)
            high = product.astype(jnp.bfloat16)
            low = (product - high.astype(jnp.float32)).astype(jnp.bfloat16)
            sums = dot_last(ones, high) + dot_last(ones, low)
            d_out[p, i:i + 1, 0:rows] = sums[0:1]
        return carry

    lax.fori_loop(0, n_head, delta_of, 0)

    def delta_copy(r):
        return pltpu.make_async_remote_copy(
            src_ref=d_out.at[peers[r]], dst_ref=d_in.at[h], send_sem=d_send.at[r], recv_sem=d_recv.at[r],
            device_id=(c, peers[r]), device_id_type=MESH,
        )

    for r in range(n_head - 1):
        delta_copy(r).start()
    d_in[h] = d_out[h]

    regroup((0, 1), 0, wait)
    spread(0)
    for r in range(n_head - 1):
        delta_copy(r).wait()
    for i in range(n_head):
        delta[:, i * rows:(i + 1) * rows] = d_in[i, :, 0:rows]

    bars = []
    for o in range(BLOCKS):
        listed = list_ref[0, 0] == c - o
        for e in range(1, list_ref.shape[1]):
            listed = listed | (list_ref[0, e] == c - o)
        bars.append(jnp.where(listed & (c - o >= 0), 0.0, jnp.inf).astype(jnp.float32))

    def one_head(i, carry):
        j = i // width
        w = i - j * width
        cols = pl.ds(pl.multiple_of(w * HEAD_SIZE, HEAD_SIZE), HEAD_SIZE)

        @pl.when(w == 0)
        def _():
            for o in range(BLOCKS):
                kt[o] = kvb[j, o, 0].T

        q = qb[j, :, cols]
        g = gb[j, :, cols]
        peak = None
        for o in range(BLOCKS):
            s = dot_last(kvb[j, o, 0], q) * (scale * LOG2E)
            sc[o] = s
            top = jnp.max(s, axis=0, keepdims=True) - bars[o]
            peak = top if peak is None else jnp.maximum(peak, top)
        total = jnp.zeros_like(peak)
        for o in range(BLOCKS):
            e = jnp.exp2(sc[o] - (peak + bars[o]))
            sc[o] = e
            total += jnp.sum(e, axis=0, keepdims=True)
        share = 1.0 / total
        row = delta[pl.ds(i, 1), :]
        dq_t = jnp.zeros((HEAD_SIZE, tokens), jnp.float32)
        for o in range(BLOCKS):
            p = sc[o] * share
            acc[j, o, 1] += dot(p.astype(jnp.bfloat16), g)
            ds = (p * (dot_last(kvb[j, o, 1], g) - row)).astype(jnp.bfloat16)
            acc[j, o, 0] += dot(ds, q)
            dq_t += dot(kt[o], ds)
        out_cols = pl.ds(pl.multiple_of(i * HEAD_SIZE, HEAD_SIZE), HEAD_SIZE)
        dq_ref[:, out_cols] = (dq_t * scale).T.astype(jnp.bfloat16)
        return carry

    for j in range(kv_count):
        if j > 0:
            regroup((0, 1), j, wait)
            spread(j)
        if j + 1 < kv_count:
            regroup((2, 3), j + 1, start)
        regroup((2, 3), j, wait)

        def step(i, carry):
            if j > 0:
                @pl.when(i == j * width + width // 3)
                def _():
                    back_two(j - 1)

                @pl.when(i == j * width + 2 * width // 3)
                def _():
                    back_three(j - 1)

            return one_head(i, carry)

        lax.fori_loop(j * width, (j + 1) * width, step, 0)
        back_one(j)
        if j > 0:
            back_four(j - 1)
    back_two(kv_count - 1)
    back_three(kv_count - 1)
    back_four(kv_count - 1)


def on_device(n_ctx, n_head, queries, keys, values, outputs, out_grad, frame_lists):
    rows = queries.shape[0]
    tokens = rows * n_head
    kv_count = keys.shape[1] // HEAD_SIZE // n_head
    heads = queries.shape[1] // HEAD_SIZE // n_head
    width = heads // kv_count
    padded = -(-heads // 16) * 16
    assert tokens == FRAME and n_ctx % 2 == 0
    bf, f32 = jnp.bfloat16, jnp.float32
    any_spec = pl.BlockSpec(memory_space=pl.ANY)
    vmem = pl.BlockSpec(memory_space=pltpu.VMEM)
    dma = pltpu.SemaphoreType.DMA
    return pl.pallas_call(
        functools.partial(kernel, n_ctx, n_head, kv_count, width),
        out_shape=(
            jax.ShapeDtypeStruct((tokens, heads * HEAD_SIZE), bf),
            jax.ShapeDtypeStruct((tokens, kv_count * HEAD_SIZE), bf),
            jax.ShapeDtypeStruct((tokens, kv_count * HEAD_SIZE), bf),
        ),
        in_specs=[any_spec] * 5 + [pl.BlockSpec(memory_space=pltpu.SMEM)],
        out_specs=(vmem, vmem, vmem),
        scratch_shapes=[
            pltpu.VMEM((kv_count, tokens, width * HEAD_SIZE), bf),
            pltpu.VMEM((kv_count, tokens, width * HEAD_SIZE), bf),
            pltpu.VMEM((kv_count, BLOCKS, 2, tokens, HEAD_SIZE), bf),
            pltpu.VMEM((BLOCKS, HEAD_SIZE, tokens), bf),
            pltpu.VMEM(out_grad.shape, bf),
            pltpu.VMEM(outputs.shape, bf),
            pltpu.VMEM((n_head, padded, HEAD_SIZE), f32),
            pltpu.VMEM((n_head, padded, HEAD_SIZE), f32),
            pltpu.VMEM((padded, tokens), f32),
            pltpu.VMEM((BLOCKS, tokens, tokens), f32),
            pltpu.VMEM((kv_count, BLOCKS, 2, tokens, HEAD_SIZE), f32),
            pltpu.VMEM((kv_count, 4, 2, tokens, HEAD_SIZE), bf),
            pltpu.VMEM((kv_count, 4, 2, tokens, HEAD_SIZE), bf),
            dma((kv_count, 4)),
            dma((2,)),
            dma((n_head - 1, kv_count, 4)),
            dma((n_head - 1, kv_count, 4)),
            dma((n_head - 1,)),
            dma((n_head - 1,)),
            dma((kv_count, 4)),
            dma((kv_count, 4)),
            dma((kv_count, 4)),
            dma((kv_count, 4)),
        ],
        compiler_params=pltpu.CompilerParams(
            collective_id=0, has_side_effects=True, vmem_limit_bytes=40 * 1024 * 1024
        ),
    )(queries, keys, values, outputs, out_grad, frame_lists)


def solution(mesh):
    split = P(("ctx", "head"), None)
    return jax.shard_map(
        functools.partial(on_device, mesh.shape["ctx"], mesh.shape["head"]),
        mesh=mesh,
        in_specs=(split,) * 5 + (P("ctx", None),),
        out_specs=(P("ctx", "head"),) * 3,
        check_vma=False,
    )
```

```python
import functools

import jax
import jax.numpy as jnp
from jax import lax
from jax.experimental import pallas as pl
from jax.experimental.pallas import tpu as pltpu
from jax.sharding import PartitionSpec as P

MESH = pl.DeviceIdType.MESH
HEAD_SIZE = 128
FRAME = 256
REACH = 4
BLOCKS = REACH + 1
LOG2E = 1.4426950408889634
LAST = (((1,), (1,)), ((), ()))


def dot(a, b):
    return jnp.dot(a, b, preferred_element_type=jnp.float32)


def dot_last(a, b):
    return lax.dot_general(a, b, LAST, preferred_element_type=jnp.float32)


def kernel(
    n_ctx, n_head, kv_count, width,
    q_ref, k_ref, v_ref, o_ref, g_ref, list_ref,
    dq_ref, dk_ref, dv_ref,
    qb, gb, kvb, g_loc, o_loc, lists, d_out, d_in, delta, sc, share, dq_sum, acc, out_buf, in_buf,
    own_sem, in_sem, a_send, a_recv, d_send, d_recv, f_send, f_recv, r_send, r_recv,
):
    c = lax.axis_index("ctx")
    h = lax.axis_index("head")
    y = lax.rem(c, 2)
    across = c + 1 - 2 * y
    rows = q_ref.shape[0]
    tokens = rows * n_head
    heads = kv_count * width
    scale = HEAD_SIZE ** -0.5

    g_in = pltpu.make_async_copy(g_ref, g_loc, in_sem.at[0])
    o_in = pltpu.make_async_copy(o_ref, o_loc, in_sem.at[1])
    l_in = pltpu.make_async_copy(list_ref, lists, in_sem.at[2])
    g_in.start()
    o_in.start()
    l_in.start()

    barrier = pltpu.get_barrier_semaphore()
    peers = [lax.rem(h + r, n_head) for r in range(1, n_head)]
    for p in peers:
        pl.semaphore_signal(barrier, inc=1, device_id=(c, p), device_id_type=MESH)
    pl.semaphore_signal(barrier, inc=1, device_id=(across, h), device_id_type=MESH)

    @pl.when(c + 2 < n_ctx)
    def _():
        pl.semaphore_signal(barrier, inc=1, device_id=(c + 2, h), device_id_type=MESH)

    @pl.when(c >= 2)
    def _():
        pl.semaphore_signal(barrier, inc=1, device_id=(c - 2, h), device_id_type=MESH)

    ends = jnp.where(c + 2 < n_ctx, 1, 0) + jnp.where(c >= 2, 1, 0)
    pl.semaphore_wait(barrier, n_head + ends)

    my_rows = pl.ds(pl.multiple_of(h * rows, rows), rows)

    def piece(what, j, p):
        if what < 2:
            start = pl.multiple_of((p * kv_count + j) * HEAD_SIZE, HEAD_SIZE)
            ref = (k_ref, v_ref)[what]
            return ref.at[:, pl.ds(start, HEAD_SIZE)], kvb.at[j, 0, what, my_rows, :]
        span = width * HEAD_SIZE
        start = pl.multiple_of((p * kv_count + j) * span, HEAD_SIZE)
        ref, place = ((q_ref, qb), (g_ref, gb))[what - 2]
        return ref.at[:, pl.ds(start, span)], place.at[j, my_rows, :]

    def remote(what, j, r):
        source, place = piece(what, j, peers[r])
        return pltpu.make_async_remote_copy(
            src_ref=source, dst_ref=place, send_sem=a_send.at[r, j, what], recv_sem=a_recv.at[r, j, what],
            device_id=(c, peers[r]), device_id_type=MESH,
        )

    def local(what, j):
        source, place = piece(what, j, h)
        return pltpu.make_async_copy(source, place, own_sem.at[j, what])

    def regroup(whats, j, do):
        for what in whats:
            for r in range(n_head - 1):
                do(remote(what, j, r))
            do(local(what, j))

    def start(copy):
        copy.start()

    def wait(copy):
        copy.wait()

    def forward(j, k):
        source, slot, target, holds = (
            (0, 2, c + 2, c + 2 < n_ctx),
            (2 * y, 1, across, c >= 2 * y),
            (2, 4, c + 2, (c + 2 < n_ctx) & (c >= 2)),
            (2 + 2 * y, 3, across, c >= 2 + 2 * y),
        )[k]
        copy = pltpu.make_async_remote_copy(
            src_ref=kvb.at[j, source], dst_ref=kvb.at[j, slot], send_sem=f_send.at[j, k],
            recv_sem=f_recv.at[j, k], device_id=(target, h), device_id_type=MESH,
        )
        return copy, holds

    def forward_start(j, k):
        copy, holds = forward(j, k)

        @pl.when(holds)
        def _():
            copy.start()

    def forward_sent(j, k):
        copy, holds = forward(j, k)

        @pl.when(holds)
        def _():
            copy.wait_send()

    def forward_here(j, k):
        copy, _ = forward(j, k)

        @pl.when(c >= (2, 1, 4, 3)[k])
        def _():
            copy.wait_recv()

    def spread(j, stage):
        if stage == 0:
            forward_start(j, 0)

            @pl.when(y == 0)
            def _():
                forward(j, 1)[0].start()
        elif stage == 1:
            forward_here(j, 0)
            forward_start(j, 2)

            @pl.when((y == 1) & (c >= 2))
            def _():
                forward(j, 1)[0].start()

            @pl.when((y == 0) & (c >= 2))
            def _():
                forward(j, 3)[0].start()
        elif stage == 2:
            forward_here(j, 2)

            @pl.when((y == 1) & (c >= 4))
            def _():
                forward(j, 3)[0].start()
        else:
            forward_here(j, 1)
            forward_here(j, 3)
            for k in range(4):
                forward_sent(j, k)

    def back(j, k):
        source, target, holds, comes = (
            (0, across, c >= 1, across >= 1),
            (1, across, c >= 3, across >= 3),
            (2, c - 2, c >= 4, (c >= 2) & (c + 2 < n_ctx)),
            (3, c - 2, c >= 2, c + 2 < n_ctx),
        )[k]
        copy = pltpu.make_async_remote_copy(
            src_ref=out_buf.at[j, source], dst_ref=in_buf.at[j, k], send_sem=r_send.at[j, k],
            recv_sem=r_recv.at[j, k], device_id=(target, h), device_id_type=MESH,
        )
        return copy, holds, comes

    def back_start(j, k, slot):
        copy, holds, _ = back(j, k)

        @pl.when(holds)
        def _():
            out_buf[j, k] = acc[j, slot].astype(jnp.bfloat16)
            copy.start()

    def back_add(j, k, slot):
        copy, _, comes = back(j, k)

        @pl.when(comes)
        def _():
            copy.wait_recv()
            acc[j, slot] += in_buf[j, k].astype(jnp.float32)

    def back_after(j, t):
        if t == 0:
            back_start(j, 1, 3)
        elif t == 1:
            back_start(j, 0, 1)
        elif t == 2:
            @pl.when(y == 0)
            def _():
                back_start(j, 2, 4)
        elif t == 3:
            @pl.when(y == 1)
            def _():
                back_add(j, 1, 4)
                back_start(j, 2, 4)

    def back_late(j):
        @pl.when(y == 0)
        def _():
            back_add(j, 1, 2)
        back_add(j, 0, 2 * y)
        back_add(j, 2, 2)
        back_start(j, 3, 2)

    def back_end(j):
        back_add(j, 3, 0)
        cols = slice(j * HEAD_SIZE, (j + 1) * HEAD_SIZE)
        dk_ref[:, cols] = (acc[j, 0, 0] * scale).astype(jnp.bfloat16)
        dv_ref[:, cols] = acc[j, 0, 1].astype(jnp.bfloat16)
        for k in range(4):
            copy, holds, _ = back(j, k)

            @pl.when(holds)
            def _():
                copy.wait_send()

    regroup((0, 1), 0, start)
    regroup((2, 3), 0, start)
    for j in range(1, kv_count):
        regroup((0, 1), j, start)

    for o in range(1, BLOCKS):
        @pl.when(c < o)
        def _():
            kvb[:, o] = jnp.zeros((kv_count, 2, tokens, HEAD_SIZE), jnp.bfloat16)
    regroup((0, 1), 0, wait)
    spread(0, 0)

    d_out[...] = jnp.zeros(d_out.shape, jnp.float32)
    g_in.wait()
    o_in.wait()
    l_in.wait()
    ones = jnp.ones((16, HEAD_SIZE), jnp.bfloat16)

    def delta_of(p, carry):
        for i in range(heads):
            cols = pl.ds(pl.multiple_of((p * heads + i) * HEAD_SIZE, HEAD_SIZE), HEAD_SIZE)
            product = g_loc[:, cols].astype(jnp.float32) * o_loc[:, cols].astype(jnp.float32)
            high = product.astype(jnp.bfloat16)
            low = (product - high.astype(jnp.float32)).astype(jnp.bfloat16)
            sums = dot_last(ones, high) + dot_last(ones, low)
            d_out[p, i:i + 1, 0:rows] = sums[0:1]
        return carry

    lax.fori_loop(0, n_head, delta_of, 0)

    def delta_copy(r):
        return pltpu.make_async_remote_copy(
            src_ref=d_out.at[peers[r]], dst_ref=d_in.at[h], send_sem=d_send.at[r], recv_sem=d_recv.at[r],
            device_id=(c, peers[r]), device_id_type=MESH,
        )

    for r in range(n_head - 1):
        delta_copy(r).start()
    d_in[h] = d_out[h]

    spread(0, 1)
    if kv_count > 1:
        regroup((2, 3), 1, start)
    spread(0, 2)
    spread(0, 3)
    for r in range(n_head - 1):
        delta_copy(r).wait()
    for i in range(n_head):
        delta[:, i * rows:(i + 1) * rows] = d_in[i, :, 0:rows]

    bars = []
    for o in range(BLOCKS):
        listed = lists[0, 0] == c - o
        for e in range(1, lists.shape[1]):
            listed = listed | (lists[0, e] == c - o)
        bars.append(jnp.where(listed & (c - o >= 0), 0.0, jnp.inf).astype(jnp.float32))

    def span(w):
        return pl.ds(pl.multiple_of(w * HEAD_SIZE, HEAD_SIZE), HEAD_SIZE)

    def exponentials(j, w):
        q = qb[j, :, span(w)]
        peak = None
        for o in range(BLOCKS):
            s = dot_last(kvb[j, o, 0], q) * (scale * LOG2E)
            sc[w, o] = s
            top = jnp.max(s, axis=0, keepdims=True) - bars[o]
            peak = top if peak is None else jnp.maximum(peak, top)
        total = jnp.zeros_like(peak)
        for o in range(BLOCKS):
            e = jnp.exp2(sc[w, o] - (peak + bars[o]))
            sc[w, o] = e
            total += jnp.sum(e, axis=0, keepdims=True)
        share[pl.ds(w, 1), :] = 1.0 / total
        dq_sum[w] = jnp.zeros(dq_sum.shape[1:], jnp.float32)

    def gradients(j, o):
        value = kvb[j, o, 1]
        key_t = kvb[j, o, 0].T
        dk = dv = None
        for w in range(width):
            cols = slice(w * HEAD_SIZE, (w + 1) * HEAD_SIZE)
            q = qb[j, :, cols]
            g = gb[j, :, cols]
            row = delta[j * width + w:j * width + w + 1, :]
            p = sc[w, o] * share[w:w + 1, :]
            ds = (p * (dot_last(value, g) - row)).astype(jnp.bfloat16)
            dv_term = dot(p.astype(jnp.bfloat16), g)
            dk_term = dot(ds, q)
            dq_sum[w] += dot(key_t, ds)
            dv = dv_term if dv is None else dv + dv_term
            dk = dk_term if dk is None else dk + dk_term
        acc[j, o, 0] = dk
        acc[j, o, 1] = dv

    for j in range(kv_count):
        regroup((2, 3), j, wait)
        hooks = {}
        if j > 0:
            hooks[width // 3] = [functools.partial(back_late, j - 1)]
            hooks[2 * width // 3] = [functools.partial(back_end, j - 1)]
        if j + 1 < kv_count:
            for stage in range(3):
                hooks.setdefault(2 * stage, []).append(functools.partial(spread, j + 1, stage))
            hooks[0].insert(0, functools.partial(regroup, (0, 1), j + 1, wait))
            if j > 0:
                hooks[0].insert(0, functools.partial(regroup, (2, 3), j + 1, start))

        def first(w, carry):
            for at, calls in hooks.items():
                @pl.when(w == at)
                def _():
                    for call in calls:
                        call()
            exponentials(j, w)
            return carry

        lax.fori_loop(0, width, first, 0)

        def second(t, carry):
            gradients(j, lax.rem(3 + 3 * t, BLOCKS))
            for at in range(4):
                @pl.when(t == at)
                def _():
                    back_after(j, at)
            return carry

        lax.fori_loop(0, BLOCKS, second, 0)
        if j + 1 < kv_count:
            spread(j + 1, 3)
        else:
            back_late(j)
        for w in range(width):
            i = j * width + w
            dq_ref[:, i * HEAD_SIZE:(i + 1) * HEAD_SIZE] = (dq_sum[w] * scale).T.astype(jnp.bfloat16)
    back_end(kv_count - 1)


def on_device(n_ctx, n_head, queries, keys, values, outputs, out_grad, frame_lists):
    rows = queries.shape[0]
    tokens = rows * n_head
    kv_count = keys.shape[1] // HEAD_SIZE // n_head
    heads = queries.shape[1] // HEAD_SIZE // n_head
    width = heads // kv_count
    padded = -(-heads // 16) * 16
    assert tokens == FRAME and n_ctx % 2 == 0
    bf, f32 = jnp.bfloat16, jnp.float32
    any_spec = pl.BlockSpec(memory_space=pl.ANY)
    vmem = pl.BlockSpec(memory_space=pltpu.VMEM)
    dma = pltpu.SemaphoreType.DMA
    return pl.pallas_call(
        functools.partial(kernel, n_ctx, n_head, kv_count, width),
        out_shape=(
            jax.ShapeDtypeStruct((tokens, heads * HEAD_SIZE), bf),
            jax.ShapeDtypeStruct((tokens, kv_count * HEAD_SIZE), bf),
            jax.ShapeDtypeStruct((tokens, kv_count * HEAD_SIZE), bf),
        ),
        in_specs=[any_spec] * 6,
        out_specs=(vmem, vmem, vmem),
        scratch_shapes=[
            pltpu.VMEM((kv_count, tokens, width * HEAD_SIZE), bf),
            pltpu.VMEM((kv_count, tokens, width * HEAD_SIZE), bf),
            pltpu.VMEM((kv_count, BLOCKS, 2, tokens, HEAD_SIZE), bf),
            pltpu.VMEM(out_grad.shape, bf),
            pltpu.VMEM(outputs.shape, bf),
            pltpu.SMEM(frame_lists.shape, jnp.int32),
            pltpu.VMEM((n_head, padded, HEAD_SIZE), f32),
            pltpu.VMEM((n_head, padded, HEAD_SIZE), f32),
            pltpu.VMEM((padded, tokens), f32),
            pltpu.VMEM((width, BLOCKS, tokens, tokens), f32),
            pltpu.VMEM((-(-width // 8) * 8, tokens), f32),
            pltpu.VMEM((width, HEAD_SIZE, tokens), f32),
            pltpu.VMEM((kv_count, BLOCKS, 2, tokens, HEAD_SIZE), f32),
            pltpu.VMEM((kv_count, 4, 2, tokens, HEAD_SIZE), bf),
            pltpu.VMEM((kv_count, 4, 2, tokens, HEAD_SIZE), bf),
            dma((kv_count, 4)),
            dma((3,)),
            dma((n_head - 1, kv_count, 4)),
            dma((n_head - 1, kv_count, 4)),
            dma((n_head - 1,)),
            dma((n_head - 1,)),
            dma((kv_count, 4)),
            dma((kv_count, 4)),
            dma((kv_count, 4)),
            dma((kv_count, 4)),
        ],
        compiler_params=pltpu.CompilerParams(
            collective_id=0, has_side_effects=True, vmem_limit_bytes=60 * 1024 * 1024
        ),
    )(queries, keys, values, outputs, out_grad, frame_lists)


def solution(mesh):
    split = P(("ctx", "head"), None)
    return jax.shard_map(
        functools.partial(on_device, mesh.shape["ctx"], mesh.shape["head"]),
        mesh=mesh,
        in_specs=(split,) * 5 + (P("ctx", None),),
        out_specs=(P("ctx", "head"),) * 3,
        check_vma=False,
    )
```

```python
import functools

import jax
import jax.numpy as jnp
from jax import lax
from jax.experimental import pallas as pl
from jax.experimental.pallas import tpu as pltpu
from jax.sharding import PartitionSpec as P

MESH = pl.DeviceIdType.MESH
HEAD_SIZE = 128
FRAME = 256
REACH = 4
BLOCKS = REACH + 1
LOG2E = 1.4426950408889634
LAST = (((1,), (1,)), ((), ()))


def dot(a, b):
    return jnp.dot(a, b, preferred_element_type=jnp.float32)


def dot_last(a, b):
    return lax.dot_general(a, b, LAST, preferred_element_type=jnp.float32)


def kernel(
    n_ctx, n_head, kv_count, width,
    q_ref, k_ref, v_ref, o_ref, g_ref, list_ref,
    dq_ref, dk_ref, dv_ref,
    qb, gb, kvb, g_loc, o_loc, lists, d_out, d_in, delta, sc, share, dq_sum, acc, out_buf, in_buf,
    own_sem, in_sem, a_send, a_recv, d_send, d_recv, f_send, f_recv, r_send, r_recv,
):
    c = lax.axis_index("ctx")
    h = lax.axis_index("head")
    y = lax.rem(c, 2)
    across = c + 1 - 2 * y
    rows = q_ref.shape[0]
    tokens = rows * n_head
    heads = kv_count * width
    scale = HEAD_SIZE ** -0.5

    g_in = pltpu.make_async_copy(g_ref, g_loc, in_sem.at[0])
    o_in = pltpu.make_async_copy(o_ref, o_loc, in_sem.at[1])
    l_in = pltpu.make_async_copy(list_ref, lists, in_sem.at[2])
    g_in.start()
    o_in.start()
    l_in.start()

    barrier = pltpu.get_barrier_semaphore()
    peers = [lax.rem(h + r, n_head) for r in range(1, n_head)]
    for p in peers:
        pl.semaphore_signal(barrier, inc=1, device_id=(c, p), device_id_type=MESH)
    pl.semaphore_signal(barrier, inc=1, device_id=(across, h), device_id_type=MESH)

    @pl.when(c + 2 < n_ctx)
    def _():
        pl.semaphore_signal(barrier, inc=1, device_id=(c + 2, h), device_id_type=MESH)

    @pl.when(c >= 2)
    def _():
        pl.semaphore_signal(barrier, inc=1, device_id=(c - 2, h), device_id_type=MESH)

    ends = jnp.where(c + 2 < n_ctx, 1, 0) + jnp.where(c >= 2, 1, 0)
    pl.semaphore_wait(barrier, n_head + ends)

    my_rows = pl.ds(pl.multiple_of(h * rows, rows), rows)

    def piece(what, j, p):
        if what < 2:
            start = pl.multiple_of((p * kv_count + j) * HEAD_SIZE, HEAD_SIZE)
            ref = (k_ref, v_ref)[what]
            return ref.at[:, pl.ds(start, HEAD_SIZE)], kvb.at[j, 0, what, my_rows, :]
        span = width * HEAD_SIZE
        start = pl.multiple_of((p * kv_count + j) * span, HEAD_SIZE)
        ref, place = ((q_ref, qb), (g_ref, gb))[what - 2]
        return ref.at[:, pl.ds(start, span)], place.at[j, my_rows, :]

    def remote(what, j, r):
        source, place = piece(what, j, peers[r])
        return pltpu.make_async_remote_copy(
            src_ref=source, dst_ref=place, send_sem=a_send.at[r, j, what], recv_sem=a_recv.at[r, j, what],
            device_id=(c, peers[r]), device_id_type=MESH,
        )

    def local(what, j):
        source, place = piece(what, j, h)
        return pltpu.make_async_copy(source, place, own_sem.at[j, what])

    def regroup(whats, j, do):
        for what in whats:
            for r in range(n_head - 1):
                do(remote(what, j, r))
            do(local(what, j))

    def start(copy):
        copy.start()

    def wait(copy):
        copy.wait()

    def forward(j, what, k):
        source, slot, target, holds = (
            (0, 2, c + 2, c + 2 < n_ctx),
            (2 * y, 1, across, c >= 2 * y),
            (2, 4, c + 2, (c + 2 < n_ctx) & (c >= 2)),
            (2 + 2 * y, 3, across, c >= 2 + 2 * y),
        )[k]
        copy = pltpu.make_async_remote_copy(
            src_ref=kvb.at[j, source, what], dst_ref=kvb.at[j, slot, what], send_sem=f_send.at[j, what, k],
            recv_sem=f_recv.at[j, what, k], device_id=(target, h), device_id_type=MESH,
        )
        return copy, holds

    def forward_start(j, what, k):
        copy, holds = forward(j, what, k)

        @pl.when(holds)
        def _():
            copy.start()

    def forward_sent(j, what, k):
        copy, holds = forward(j, what, k)

        @pl.when(holds)
        def _():
            copy.wait_send()

    def forward_here(j, what, k):
        copy, _ = forward(j, what, k)

        @pl.when(c >= (2, 1, 4, 3)[k])
        def _():
            copy.wait_recv()

    def spread(j, what, stage):
        if stage == 0:
            forward_start(j, what, 0)

            @pl.when(y == 0)
            def _():
                forward(j, what, 1)[0].start()
        elif stage == 1:
            forward_here(j, what, 0)
            forward_start(j, what, 2)

            @pl.when((y == 1) & (c >= 2))
            def _():
                forward(j, what, 1)[0].start()

            @pl.when((y == 0) & (c >= 2))
            def _():
                forward(j, what, 3)[0].start()
        elif stage == 2:
            forward_here(j, what, 2)

            @pl.when((y == 1) & (c >= 4))
            def _():
                forward(j, what, 3)[0].start()
        else:
            forward_here(j, what, 1)
            forward_here(j, what, 3)
            for k in range(4):
                forward_sent(j, what, k)

    def back(j, k):
        source, target, holds, comes = (
            (0, across, c >= 1, across >= 1),
            (1, across, c >= 3, across >= 3),
            (2, c - 2, c >= 4, (c >= 2) & (c + 2 < n_ctx)),
            (3, c - 2, c >= 2, c + 2 < n_ctx),
        )[k]
        copy = pltpu.make_async_remote_copy(
            src_ref=out_buf.at[j, source], dst_ref=in_buf.at[j, k], send_sem=r_send.at[j, k],
            recv_sem=r_recv.at[j, k], device_id=(target, h), device_id_type=MESH,
        )
        return copy, holds, comes

    def back_start(j, k, slot):
        copy, holds, _ = back(j, k)

        @pl.when(holds)
        def _():
            out_buf[j, k] = acc[j, slot].astype(jnp.bfloat16)
            copy.start()

    def back_add(j, k, slot):
        copy, _, comes = back(j, k)

        @pl.when(comes)
        def _():
            copy.wait_recv()
            acc[j, slot] += in_buf[j, k].astype(jnp.float32)

    def back_after(j, t):
        if t == 0:
            back_start(j, 1, 3)
            back_start(j, 0, 1)
        elif t == 1:
            back_add(j, 1, 2 + 2 * y)
            back_start(j, 2, 4)

    def back_late(j):
        back_add(j, 0, 2 * y)
        back_add(j, 2, 2)
        back_start(j, 3, 2)

    def back_end(j):
        back_add(j, 3, 0)
        cols = slice(j * HEAD_SIZE, (j + 1) * HEAD_SIZE)
        dk_ref[:, cols] = (acc[j, 0, 0] * scale).astype(jnp.bfloat16)
        dv_ref[:, cols] = acc[j, 0, 1].astype(jnp.bfloat16)
        for k in range(4):
            copy, holds, _ = back(j, k)

            @pl.when(holds)
            def _():
                copy.wait_send()

    for what in (0, 2, 1, 3):
        regroup((what,), 0, start)

    for o in range(1, BLOCKS):
        @pl.when(c < o)
        def _():
            kvb[:, o] = jnp.zeros((kv_count, 2, tokens, HEAD_SIZE), jnp.bfloat16)
    regroup((0,), 0, wait)
    spread(0, 0, 0)

    d_out[...] = jnp.zeros(d_out.shape, jnp.float32)
    g_in.wait()
    o_in.wait()
    l_in.wait()
    ones = jnp.ones((16, HEAD_SIZE), jnp.bfloat16)

    def delta_of(p, carry):
        for i in range(heads):
            cols = pl.ds(pl.multiple_of((p * heads + i) * HEAD_SIZE, HEAD_SIZE), HEAD_SIZE)
            product = g_loc[:, cols].astype(jnp.float32) * o_loc[:, cols].astype(jnp.float32)
            high = product.astype(jnp.bfloat16)
            low = (product - high.astype(jnp.float32)).astype(jnp.bfloat16)
            sums = dot_last(ones, high) + dot_last(ones, low)
            d_out[p, i:i + 1, 0:rows] = sums[0:1]
        return carry

    lax.fori_loop(0, n_head, delta_of, 0)

    def delta_copy(r):
        return pltpu.make_async_remote_copy(
            src_ref=d_out.at[peers[r]], dst_ref=d_in.at[h], send_sem=d_send.at[r], recv_sem=d_recv.at[r],
            device_id=(c, peers[r]), device_id_type=MESH,
        )

    for r in range(n_head - 1):
        delta_copy(r).start()
    d_in[h] = d_out[h]

    spread(0, 0, 1)
    if kv_count > 1:
        regroup((0, 2), 1, start)
    spread(0, 0, 2)
    spread(0, 0, 3)
    for r in range(n_head - 1):
        delta_copy(r).wait()
    for i in range(n_head):
        delta[:, i * rows:(i + 1) * rows] = d_in[i, :, 0:rows]

    bars = []
    for o in range(BLOCKS):
        listed = lists[0, 0] == c - o
        for e in range(1, lists.shape[1]):
            listed = listed | (lists[0, e] == c - o)
        bars.append(jnp.where(listed & (c - o >= 0), 0.0, jnp.inf).astype(jnp.float32))

    def score(j, w, o):
        s = dot_last(kvb[j, o, 0], qb[j, :, w * HEAD_SIZE:(w + 1) * HEAD_SIZE]) * (scale * LOG2E)
        sc[w, o] = s
        return jnp.max(s, axis=0, keepdims=True) - bars[o]

    def exponential(w, o, peak):
        e = jnp.exp2(sc[w, o] - (peak + bars[o]))
        sc[w, o] = e
        return jnp.sum(e, axis=0, keepdims=True)

    def gradients(j, blocks):
        values = jnp.concatenate([kvb[j, o, 1] for o in blocks], axis=0)
        keys_t = jnp.concatenate([kvb[j, o, 0] for o in blocks], axis=0).T
        dk = dv = None
        for w in range(width):
            cols = slice(w * HEAD_SIZE, (w + 1) * HEAD_SIZE)
            q = qb[j, :, cols]
            g = gb[j, :, cols]
            row = delta[j * width + w:j * width + w + 1, :]
            p = jnp.concatenate([sc[w, o] for o in blocks], axis=0) * share[w:w + 1, :]
            ds = (p * (dot_last(values, g) - row)).astype(jnp.bfloat16)
            dv_term = dot(p.astype(jnp.bfloat16), g)
            dk_term = dot(ds, q)
            dq_term = dot(keys_t, ds)
            dq_sum[w] = dq_term if blocks is plan[0] else dq_sum[w] + dq_term
            dv = dv_term if dv is None else dv + dv_term
            dk = dk_term if dk is None else dk + dk_term
        for at, o in enumerate(blocks):
            acc[j, o, 0] = dk[at * tokens:(at + 1) * tokens]
            acc[j, o, 1] = dv[at * tokens:(at + 1) * tokens]

    plan = ((3, 1), (4, 2), (0,))

    for j in range(kv_count):
        more = j + 1 < kv_count
        regroup((2,), j, wait)
        peak = None
        for w in range(-1, width):
            if w == 0:
                regroup((1,), j, wait)
                spread(j, 1, 0)
            if w == width // 3:
                spread(j, 1, 1)
                if j > 0:
                    back_late(j - 1)
            if w == 2 * width // 3:
                spread(j, 1, 2)
                if j > 0:
                    back_end(j - 1)
            tops, total = None, 0.0
            for o in range(BLOCKS):
                if w + 1 < width:
                    top = score(j, w + 1, o)
                    tops = top if tops is None else jnp.maximum(tops, top)
                if w >= 0:
                    total += exponential(w, o, peak)
            if w >= 0:
                share[w:w + 1, :] = 1.0 / total
            peak = tops
        spread(j, 1, 3)
        regroup((3,), j, wait)
        if more:
            regroup((1, 3), j + 1, start)
            regroup((0,), j + 1, wait)
            spread(j + 1, 0, 0)
        for t, blocks in enumerate(plan):
            gradients(j, blocks)
            back_after(j, t)
            if more:
                spread(j + 1, 0, t + 1)
            elif t == 2:
                back_late(j)
        for w in range(width):
            i = j * width + w
            dq_ref[:, i * HEAD_SIZE:(i + 1) * HEAD_SIZE] = (dq_sum[w] * scale).T.astype(jnp.bfloat16)
        if j + 2 < kv_count:
            regroup((0, 2), j + 2, start)
    back_end(kv_count - 1)


def hand_over(*refs):
    sems = refs[-1]
    count = (len(refs) - 1) // 2
    copies = [pltpu.make_async_copy(refs[i], refs[count + i], sems.at[i]) for i in range(count)]
    for copy in copies:
        copy.start()
    for copy in copies:
        copy.wait()


def on_device(n_ctx, n_head, queries, keys, values, outputs, out_grad, frame_lists):
    rows = queries.shape[0]
    tokens = rows * n_head
    kv_count = keys.shape[1] // HEAD_SIZE // n_head
    heads = queries.shape[1] // HEAD_SIZE // n_head
    width = heads // kv_count
    padded = -(-heads // 16) * 16
    assert tokens == FRAME and n_ctx % 2 == 0
    bf, f32 = jnp.bfloat16, jnp.float32
    any_spec = pl.BlockSpec(memory_space=pl.ANY)
    vmem = pl.BlockSpec(memory_space=pltpu.VMEM)
    dma = pltpu.SemaphoreType.DMA
    results = pl.pallas_call(
        functools.partial(kernel, n_ctx, n_head, kv_count, width),
        out_shape=(
            jax.ShapeDtypeStruct((tokens, heads * HEAD_SIZE), bf),
            jax.ShapeDtypeStruct((tokens, kv_count * HEAD_SIZE), bf),
            jax.ShapeDtypeStruct((tokens, kv_count * HEAD_SIZE), bf),
        ),
        in_specs=[any_spec] * 6,
        out_specs=(vmem, vmem, vmem),
        scratch_shapes=[
            pltpu.VMEM((kv_count, tokens, width * HEAD_SIZE), bf),
            pltpu.VMEM((kv_count, tokens, width * HEAD_SIZE), bf),
            pltpu.VMEM((kv_count, BLOCKS, 2, tokens, HEAD_SIZE), bf),
            pltpu.VMEM(out_grad.shape, bf),
            pltpu.VMEM(outputs.shape, bf),
            pltpu.SMEM(frame_lists.shape, jnp.int32),
            pltpu.VMEM((n_head, padded, HEAD_SIZE), f32),
            pltpu.VMEM((n_head, padded, HEAD_SIZE), f32),
            pltpu.VMEM((padded, tokens), f32),
            pltpu.VMEM((width, BLOCKS, tokens, tokens), f32),
            pltpu.VMEM((-(-width // 8) * 8, tokens), f32),
            pltpu.VMEM((width, HEAD_SIZE, tokens), f32),
            pltpu.VMEM((kv_count, BLOCKS, 2, tokens, HEAD_SIZE), f32),
            pltpu.VMEM((kv_count, 4, 2, tokens, HEAD_SIZE), bf),
            pltpu.VMEM((kv_count, 4, 2, tokens, HEAD_SIZE), bf),
            dma((kv_count, 4)),
            dma((3,)),
            dma((n_head - 1, kv_count, 4)),
            dma((n_head - 1, kv_count, 4)),
            dma((n_head - 1,)),
            dma((n_head - 1,)),
            dma((kv_count, 2, 4)),
            dma((kv_count, 2, 4)),
            dma((kv_count, 4)),
            dma((kv_count, 4)),
        ],
        compiler_params=pltpu.CompilerParams(
            collective_id=0, has_side_effects=True, vmem_limit_bytes=60 * 1024 * 1024
        ),
    )(queries, keys, values, outputs, out_grad, frame_lists)
    return pl.pallas_call(
        hand_over,
        out_shape=[jax.ShapeDtypeStruct(x.shape, x.dtype) for x in results],
        in_specs=[any_spec] * 3,
        out_specs=[any_spec] * 3,
        scratch_shapes=[dma((3,))],
    )(*results)


def solution(mesh):
    split = P(("ctx", "head"), None)
    return jax.shard_map(
        functools.partial(on_device, mesh.shape["ctx"], mesh.shape["head"]),
        mesh=mesh,
        in_specs=(split,) * 5 + (P("ctx", None),),
        out_specs=(P("ctx", "head"),) * 3,
        check_vma=False,
    )
```

```python
import functools

import jax
import jax.numpy as jnp
from jax import lax
from jax.experimental import pallas as pl
from jax.experimental.pallas import tpu as pltpu
from jax.sharding import PartitionSpec as P

MESH = pl.DeviceIdType.MESH
HEAD_SIZE = 128
FRAME = 256
REACH = 4
BLOCKS = REACH + 1
LOG2E = 1.4426950408889634
LAST = (((1,), (1,)), ((), ()))


def dot(a, b):
    return jnp.dot(a, b, preferred_element_type=jnp.float32)


def dot_last(a, b):
    return lax.dot_general(a, b, LAST, preferred_element_type=jnp.float32)


def kernel(
    n_ctx, n_head, kv_count, width,
    q_ref, k_ref, v_ref, o_ref, g_ref, list_ref,
    dq_ref, dk_ref, dv_ref,
    qb, gb, kvb, g_loc, o_loc, lists, d_out, d_in, delta, sc, share, dq_sum, acc, out_buf, in_buf,
    own_sem, in_sem, a_send, a_recv, d_send, d_recv, f_send, f_recv, r_send, r_recv,
):
    c = lax.axis_index("ctx")
    h = lax.axis_index("head")
    y = lax.rem(c, 2)
    across = c + 1 - 2 * y
    rows = q_ref.shape[0]
    tokens = rows * n_head
    heads = kv_count * width
    scale = HEAD_SIZE ** -0.5

    g_in = pltpu.make_async_copy(g_ref, g_loc, in_sem.at[0])
    o_in = pltpu.make_async_copy(o_ref, o_loc, in_sem.at[1])
    l_in = pltpu.make_async_copy(list_ref, lists, in_sem.at[2])
    g_in.start()
    o_in.start()
    l_in.start()

    barrier = pltpu.get_barrier_semaphore()
    peers = [lax.rem(h + r, n_head) for r in range(1, n_head)]
    for p in peers:
        pl.semaphore_signal(barrier, inc=1, device_id=(c, p), device_id_type=MESH)
    pl.semaphore_signal(barrier, inc=1, device_id=(across, h), device_id_type=MESH)

    @pl.when(c + 2 < n_ctx)
    def _():
        pl.semaphore_signal(barrier, inc=1, device_id=(c + 2, h), device_id_type=MESH)

    @pl.when(c >= 2)
    def _():
        pl.semaphore_signal(barrier, inc=1, device_id=(c - 2, h), device_id_type=MESH)

    ends = jnp.where(c + 2 < n_ctx, 1, 0) + jnp.where(c >= 2, 1, 0)
    pl.semaphore_wait(barrier, n_head + ends)

    my_rows = pl.ds(pl.multiple_of(h * rows, rows), rows)

    def piece(what, j, p):
        if what < 2:
            start = pl.multiple_of((p * kv_count + j) * HEAD_SIZE, HEAD_SIZE)
            ref = (k_ref, v_ref)[what]
            return ref.at[:, pl.ds(start, HEAD_SIZE)], kvb.at[j, 0, what, my_rows, :]
        span = width * HEAD_SIZE
        start = pl.multiple_of((p * kv_count + j) * span, HEAD_SIZE)
        ref, place = ((q_ref, qb), (g_ref, gb))[what - 2]
        return ref.at[:, pl.ds(start, span)], place.at[j, my_rows, :]

    def remote(what, j, r):
        source, place = piece(what, j, peers[r])
        return pltpu.make_async_remote_copy(
            src_ref=source, dst_ref=place, send_sem=a_send.at[r, j, what], recv_sem=a_recv.at[r, j, what],
            device_id=(c, peers[r]), device_id_type=MESH,
        )

    def local(what, j):
        source, place = piece(what, j, h)
        return pltpu.make_async_copy(source, place, own_sem.at[j, what])

    def regroup(whats, j, do):
        for what in whats:
            for r in range(n_head - 1):
                do(remote(what, j, r))
            do(local(what, j))

    def start(copy):
        copy.start()

    def wait(copy):
        copy.wait()

    def forward(j, what, k):
        source, slot, target, holds = (
            (0, 2, c + 2, c + 2 < n_ctx),
            (2 * y, 1, across, c >= 2 * y),
            (2, 4, c + 2, (c + 2 < n_ctx) & (c >= 2)),
            (2 + 2 * y, 3, across, c >= 2 + 2 * y),
        )[k]
        copy = pltpu.make_async_remote_copy(
            src_ref=kvb.at[j, source, what], dst_ref=kvb.at[j, slot, what], send_sem=f_send.at[j, what, k],
            recv_sem=f_recv.at[j, what, k], device_id=(target, h), device_id_type=MESH,
        )
        return copy, holds

    def forward_start(j, what, k):
        copy, holds = forward(j, what, k)

        @pl.when(holds)
        def _():
            copy.start()

    def forward_sent(j, what, k):
        copy, holds = forward(j, what, k)

        @pl.when(holds)
        def _():
            copy.wait_send()

    def forward_here(j, what, k):
        copy, _ = forward(j, what, k)

        @pl.when(c >= (2, 1, 4, 3)[k])
        def _():
            copy.wait_recv()

    def spread(j, what, stage):
        if stage == 0:
            forward_start(j, what, 0)

            @pl.when(y == 0)
            def _():
                forward(j, what, 1)[0].start()
        elif stage == 1:
            forward_here(j, what, 0)
            forward_start(j, what, 2)

            @pl.when((y == 1) & (c >= 2))
            def _():
                forward(j, what, 1)[0].start()

            @pl.when((y == 0) & (c >= 2))
            def _():
                forward(j, what, 3)[0].start()
        elif stage == 2:
            forward_here(j, what, 2)

            @pl.when((y == 1) & (c >= 4))
            def _():
                forward(j, what, 3)[0].start()
        else:
            forward_here(j, what, 1)
            forward_here(j, what, 3)
            for k in range(4):
                forward_sent(j, what, k)

    def back(j, k):
        source, target, holds, comes = (
            (0, across, c >= 1, across >= 1),
            (1, across, c >= 3, across >= 3),
            (2, c - 2, c >= 4, (c >= 2) & (c + 2 < n_ctx)),
            (3, c - 2, c >= 2, c + 2 < n_ctx),
        )[k]
        copy = pltpu.make_async_remote_copy(
            src_ref=out_buf.at[j, source], dst_ref=in_buf.at[j, k], send_sem=r_send.at[j, k],
            recv_sem=r_recv.at[j, k], device_id=(target, h), device_id_type=MESH,
        )
        return copy, holds, comes

    def back_start(j, k, slot):
        copy, holds, _ = back(j, k)

        @pl.when(holds)
        def _():
            out_buf[j, k] = acc[j, slot].astype(jnp.bfloat16)
            copy.start()

    def back_add(j, k, slot):
        copy, _, comes = back(j, k)

        @pl.when(comes)
        def _():
            copy.wait_recv()
            acc[j, slot] += in_buf[j, k].astype(jnp.float32)

    def back_after(j, t):
        if t == 0:
            back_start(j, 1, 3)
        elif t == 1:
            back_start(j, 0, 1)
        elif t == 2:
            @pl.when(y == 0)
            def _():
                back_start(j, 2, 4)
        elif t == 3:
            @pl.when(y == 1)
            def _():
                back_add(j, 1, 4)
                back_start(j, 2, 4)

    def back_late(j):
        @pl.when(y == 0)
        def _():
            back_add(j, 1, 2)
        back_add(j, 0, 2 * y)
        back_add(j, 2, 2)
        back_start(j, 3, 2)

    def back_end(j):
        back_add(j, 3, 0)
        cols = slice(j * HEAD_SIZE, (j + 1) * HEAD_SIZE)
        dk_ref[:, cols] = (acc[j, 0, 0] * scale).astype(jnp.bfloat16)
        dv_ref[:, cols] = acc[j, 0, 1].astype(jnp.bfloat16)
        for k in range(4):
            copy, holds, _ = back(j, k)

            @pl.when(holds)
            def _():
                copy.wait_send()

    for what in (0, 2, 1, 3):
        regroup((what,), 0, start)

    for o in range(1, BLOCKS):
        @pl.when(c < o)
        def _():
            kvb[:, o] = jnp.zeros((kv_count, 2, tokens, HEAD_SIZE), jnp.bfloat16)
    regroup((0,), 0, wait)
    spread(0, 0, 0)

    d_out[...] = jnp.zeros(d_out.shape, jnp.float32)
    g_in.wait()
    o_in.wait()
    l_in.wait()
    ones = jnp.ones((16, HEAD_SIZE), jnp.bfloat16)

    def delta_of(p, carry):
        for i in range(heads):
            cols = pl.ds(pl.multiple_of((p * heads + i) * HEAD_SIZE, HEAD_SIZE), HEAD_SIZE)
            product = g_loc[:, cols].astype(jnp.float32) * o_loc[:, cols].astype(jnp.float32)
            high = product.astype(jnp.bfloat16)
            low = (product - high.astype(jnp.float32)).astype(jnp.bfloat16)
            sums = dot_last(ones, high) + dot_last(ones, low)
            d_out[p, i:i + 1, 0:rows] = sums[0:1]
        return carry

    lax.fori_loop(0, n_head, delta_of, 0)

    def delta_copy(r):
        return pltpu.make_async_remote_copy(
            src_ref=d_out.at[peers[r]], dst_ref=d_in.at[h], send_sem=d_send.at[r], recv_sem=d_recv.at[r],
            device_id=(c, peers[r]), device_id_type=MESH,
        )

    for r in range(n_head - 1):
        delta_copy(r).start()
    d_in[h] = d_out[h]

    spread(0, 0, 1)
    if kv_count > 1:
        regroup((0, 2), 1, start)
    spread(0, 0, 2)
    spread(0, 0, 3)
    for r in range(n_head - 1):
        delta_copy(r).wait()
    for i in range(n_head):
        delta[:, i * rows:(i + 1) * rows] = d_in[i, :, 0:rows]

    bars = []
    for o in range(BLOCKS):
        listed = lists[0, 0] == c - o
        for e in range(1, lists.shape[1]):
            listed = listed | (lists[0, e] == c - o)
        bars.append(jnp.where(listed & (c - o >= 0), 0.0, jnp.inf).astype(jnp.float32))

    def span(w):
        return pl.ds(pl.multiple_of(w * HEAD_SIZE, HEAD_SIZE), HEAD_SIZE)

    def exponentials(j, w):
        q = qb[j, :, span(w)]
        peak = None
        for o in range(BLOCKS):
            s = dot_last(kvb[j, o, 0], q) * (scale * LOG2E)
            sc[w, o] = s
            top = jnp.max(s, axis=0, keepdims=True) - bars[o]
            peak = top if peak is None else jnp.maximum(peak, top)
        total = jnp.zeros_like(peak)
        for o in range(BLOCKS):
            e = jnp.exp2(sc[w, o] - (peak + bars[o]))
            sc[w, o] = e
            total += jnp.sum(e, axis=0, keepdims=True)
        share[pl.ds(w, 1), :] = 1.0 / total
        dq_sum[w] = jnp.zeros(dq_sum.shape[1:], jnp.float32)

    def gradients(j, o):
        value = kvb[j, o, 1]
        key_t = kvb[j, o, 0].T
        dk = dv = None
        for w in range(width):
            cols = slice(w * HEAD_SIZE, (w + 1) * HEAD_SIZE)
            q = qb[j, :, cols]
            g = gb[j, :, cols]
            row = delta[j * width + w:j * width + w + 1, :]
            p = sc[w, o] * share[w:w + 1, :]
            ds = (p * (dot_last(value, g) - row)).astype(jnp.bfloat16)
            dv_term = dot(p.astype(jnp.bfloat16), g)
            dk_term = dot(ds, q)
            dq_sum[w] += dot(key_t, ds)
            dv = dv_term if dv is None else dv + dv_term
            dk = dk_term if dk is None else dk + dk_term
        acc[j, o, 0] = dk
        acc[j, o, 1] = dv

    third = width // 3

    for j in range(kv_count):
        more = j + 1 < kv_count
        regroup((2,), j, wait)
        regroup((1,), j, wait)
        spread(j, 1, 0)

        def first(w, carry):
            for at in (1, 2):
                @pl.when(w == at * third)
                def _():
                    spread(j, 1, at)
                    if j > 0:
                        (back_late, back_end)[at - 1](j - 1)
            exponentials(j, w)
            return carry

        lax.fori_loop(0, width, first, 0)
        spread(j, 1, 3)
        regroup((3,), j, wait)
        if more:
            regroup((1, 3), j + 1, start)
            regroup((0,), j + 1, wait)
            spread(j + 1, 0, 0)

        def second(t, carry):
            gradients(j, lax.rem(3 + 3 * t, BLOCKS))
            for at in range(4):
                @pl.when(t == at)
                def _():
                    back_after(j, at)
                    if more and 1 <= at <= 2:
                        spread(j + 1, 0, at)
            return carry

        lax.fori_loop(0, BLOCKS, second, 0)
        if more:
            spread(j + 1, 0, 3)
        else:
            back_late(j)
        for w in range(width):
            i = j * width + w
            dq_ref[:, i * HEAD_SIZE:(i + 1) * HEAD_SIZE] = (dq_sum[w] * scale).T.astype(jnp.bfloat16)
        if j + 2 < kv_count:
            regroup((0, 2), j + 2, start)
    back_end(kv_count - 1)


def hand_over(*refs):
    sems = refs[-1]
    count = (len(refs) - 1) // 2
    copies = [pltpu.make_async_copy(refs[i], refs[count + i], sems.at[i]) for i in range(count)]
    for copy in copies:
        copy.start()
    for copy in copies:
        copy.wait()


def on_device(n_ctx, n_head, queries, keys, values, outputs, out_grad, frame_lists):
    rows = queries.shape[0]
    tokens = rows * n_head
    kv_count = keys.shape[1] // HEAD_SIZE // n_head
    heads = queries.shape[1] // HEAD_SIZE // n_head
    width = heads // kv_count
    padded = -(-heads // 16) * 16
    assert tokens == FRAME and n_ctx % 2 == 0
    bf, f32 = jnp.bfloat16, jnp.float32
    any_spec = pl.BlockSpec(memory_space=pl.ANY)
    vmem = pl.BlockSpec(memory_space=pltpu.VMEM)
    dma = pltpu.SemaphoreType.DMA
    results = pl.pallas_call(
        functools.partial(kernel, n_ctx, n_head, kv_count, width),
        out_shape=(
            jax.ShapeDtypeStruct((tokens, heads * HEAD_SIZE), bf),
            jax.ShapeDtypeStruct((tokens, kv_count * HEAD_SIZE), bf),
            jax.ShapeDtypeStruct((tokens, kv_count * HEAD_SIZE), bf),
        ),
        in_specs=[any_spec] * 6,
        out_specs=(vmem, vmem, vmem),
        scratch_shapes=[
            pltpu.VMEM((kv_count, tokens, width * HEAD_SIZE), bf),
            pltpu.VMEM((kv_count, tokens, width * HEAD_SIZE), bf),
            pltpu.VMEM((kv_count, BLOCKS, 2, tokens, HEAD_SIZE), bf),
            pltpu.VMEM(out_grad.shape, bf),
            pltpu.VMEM(outputs.shape, bf),
            pltpu.SMEM(frame_lists.shape, jnp.int32),
            pltpu.VMEM((n_head, padded, HEAD_SIZE), f32),
            pltpu.VMEM((n_head, padded, HEAD_SIZE), f32),
            pltpu.VMEM((padded, tokens), f32),
            pltpu.VMEM((width, BLOCKS, tokens, tokens), f32),
            pltpu.VMEM((-(-width // 8) * 8, tokens), f32),
            pltpu.VMEM((width, HEAD_SIZE, tokens), f32),
            pltpu.VMEM((kv_count, BLOCKS, 2, tokens, HEAD_SIZE), f32),
            pltpu.VMEM((kv_count, 4, 2, tokens, HEAD_SIZE), bf),
            pltpu.VMEM((kv_count, 4, 2, tokens, HEAD_SIZE), bf),
            dma((kv_count, 4)),
            dma((3,)),
            dma((n_head - 1, kv_count, 4)),
            dma((n_head - 1, kv_count, 4)),
            dma((n_head - 1,)),
            dma((n_head - 1,)),
            dma((kv_count, 2, 4)),
            dma((kv_count, 2, 4)),
            dma((kv_count, 4)),
            dma((kv_count, 4)),
        ],
        compiler_params=pltpu.CompilerParams(
            collective_id=0, has_side_effects=True, vmem_limit_bytes=60 * 1024 * 1024
        ),
    )(queries, keys, values, outputs, out_grad, frame_lists)
    return pl.pallas_call(
        hand_over,
        out_shape=[jax.ShapeDtypeStruct(x.shape, x.dtype) for x in results],
        in_specs=[any_spec] * 3,
        out_specs=[vmem] * 3,
        scratch_shapes=[dma((3,))],
    )(*results)


def solution(mesh):
    split = P(("ctx", "head"), None)
    return jax.shard_map(
        functools.partial(on_device, mesh.shape["ctx"], mesh.shape["head"]),
        mesh=mesh,
        in_specs=(split,) * 5 + (P("ctx", None),),
        out_specs=(P("ctx", "head"),) * 3,
        check_vma=False,
    )
```

```python
import functools

import jax
import jax.numpy as jnp
from jax import lax
from jax.experimental import pallas as pl
from jax.experimental.pallas import tpu as pltpu
from jax.sharding import PartitionSpec as P

MESH = pl.DeviceIdType.MESH
HEAD_SIZE = 128
FRAME = 256
REACH = 4
BLOCKS = REACH + 1
LOG2E = 1.4426950408889634
LAST = (((1,), (1,)), ((), ()))


def dot(a, b):
    return jnp.dot(a, b, preferred_element_type=jnp.float32)


def dot_last(a, b):
    return lax.dot_general(a, b, LAST, preferred_element_type=jnp.float32)


def kernel(
    n_ctx, n_head, kv_count, width,
    q_ref, k_ref, v_ref, o_ref, g_ref, list_ref,
    dq_ref, dk_ref, dv_ref,
    qb, gb, kvb, q_loc, g_loc, o_loc, lists, d_out, d_in, delta, sc, share, dq_sum, acc, out_buf, in_buf,
    own_sem, in_sem, a_send, a_recv, d_send, d_recv, f_send, f_recv, r_send, r_recv,
):
    c = lax.axis_index("ctx")
    h = lax.axis_index("head")
    y = lax.rem(c, 2)
    across = c + 1 - 2 * y
    rows = q_ref.shape[0]
    tokens = rows * n_head
    heads = kv_count * width
    scale = HEAD_SIZE ** -0.5

    g_in = pltpu.make_async_copy(g_ref, g_loc, in_sem.at[0])
    o_in = pltpu.make_async_copy(o_ref, o_loc, in_sem.at[1])
    l_in = pltpu.make_async_copy(list_ref, lists, in_sem.at[2])
    q_in = pltpu.make_async_copy(q_ref, q_loc, in_sem.at[3])
    q_in.start()
    g_in.start()
    o_in.start()
    l_in.start()

    barrier = pltpu.get_barrier_semaphore()
    peers = [lax.rem(h + r, n_head) for r in range(1, n_head)]
    for p in peers:
        pl.semaphore_signal(barrier, inc=1, device_id=(c, p), device_id_type=MESH)
    pl.semaphore_signal(barrier, inc=1, device_id=(across, h), device_id_type=MESH)

    @pl.when(c + 2 < n_ctx)
    def _():
        pl.semaphore_signal(barrier, inc=1, device_id=(c + 2, h), device_id_type=MESH)

    @pl.when(c >= 2)
    def _():
        pl.semaphore_signal(barrier, inc=1, device_id=(c - 2, h), device_id_type=MESH)

    ends = jnp.where(c + 2 < n_ctx, 1, 0) + jnp.where(c >= 2, 1, 0)
    pl.semaphore_wait(barrier, n_head + ends)

    my_rows = pl.ds(pl.multiple_of(h * rows, rows), rows)

    def piece(what, j, p):
        if what < 2:
            start = pl.multiple_of((p * kv_count + j) * HEAD_SIZE, HEAD_SIZE)
            ref = (k_ref, v_ref)[what]
            return ref.at[:, pl.ds(start, HEAD_SIZE)], kvb.at[j, 0, what, my_rows, :]
        span = width * HEAD_SIZE
        start = pl.multiple_of((p * kv_count + j) * span, HEAD_SIZE)
        ref, place = ((q_loc, qb), (g_loc, gb))[what - 2]
        return ref.at[:, pl.ds(start, span)], place.at[j, my_rows, :]

    def remote(what, j, r):
        source, place = piece(what, j, peers[r])
        return pltpu.make_async_remote_copy(
            src_ref=source, dst_ref=place, send_sem=a_send.at[r, j, what], recv_sem=a_recv.at[r, j, what],
            device_id=(c, peers[r]), device_id_type=MESH,
        )

    def local(what, j):
        source, place = piece(what, j, h)
        return pltpu.make_async_copy(source, place, own_sem.at[j, what])

    def regroup(whats, j, do):
        for what in whats:
            for r in range(n_head - 1):
                do(remote(what, j, r))
            do(local(what, j))

    def start(copy):
        copy.start()

    def wait(copy):
        copy.wait()

    def forward(j, what, k):
        source, slot, target, holds = (
            (0, 2, c + 2, c + 2 < n_ctx),
            (2 * y, 1, across, c >= 2 * y),
            (2, 4, c + 2, (c + 2 < n_ctx) & (c >= 2)),
            (2 + 2 * y, 3, across, c >= 2 + 2 * y),
        )[k]
        copy = pltpu.make_async_remote_copy(
            src_ref=kvb.at[j, source, what], dst_ref=kvb.at[j, slot, what], send_sem=f_send.at[j, what, k],
            recv_sem=f_recv.at[j, what, k], device_id=(target, h), device_id_type=MESH,
        )
        return copy, holds

    def forward_start(j, what, k):
        copy, holds = forward(j, what, k)

        @pl.when(holds)
        def _():
            copy.start()

    def forward_sent(j, what, k):
        copy, holds = forward(j, what, k)

        @pl.when(holds)
        def _():
            copy.wait_send()

    def forward_here(j, what, k):
        copy, _ = forward(j, what, k)

        @pl.when(c >= (2, 1, 4, 3)[k])
        def _():
            copy.wait_recv()

    def spread(j, what, stage):
        if stage == 0:
            forward_start(j, what, 0)

            @pl.when(y == 0)
            def _():
                forward(j, what, 1)[0].start()
        elif stage == 1:
            forward_here(j, what, 0)
            forward_start(j, what, 2)

            @pl.when((y == 1) & (c >= 2))
            def _():
                forward(j, what, 1)[0].start()

            @pl.when((y == 0) & (c >= 2))
            def _():
                forward(j, what, 3)[0].start()
        elif stage == 2:
            forward_here(j, what, 2)

            @pl.when((y == 1) & (c >= 4))
            def _():
                forward(j, what, 3)[0].start()
        else:
            forward_here(j, what, 1)
            forward_here(j, what, 3)
            for k in range(4):
                forward_sent(j, what, k)

    def back(j, k):
        source, target, holds, comes = (
            (0, across, c >= 1, across >= 1),
            (1, across, c >= 3, across >= 3),
            (2, c - 2, c >= 4, (c >= 2) & (c + 2 < n_ctx)),
            (3, c - 2, c >= 2, c + 2 < n_ctx),
        )[k]
        copy = pltpu.make_async_remote_copy(
            src_ref=out_buf.at[j, source], dst_ref=in_buf.at[j, k], send_sem=r_send.at[j, k],
            recv_sem=r_recv.at[j, k], device_id=(target, h), device_id_type=MESH,
        )
        return copy, holds, comes

    def back_start(j, k, slot):
        copy, holds, _ = back(j, k)

        @pl.when(holds)
        def _():
            out_buf[j, k] = acc[j, slot].astype(jnp.bfloat16)
            copy.start()

    def back_add(j, k, slot):
        copy, _, comes = back(j, k)

        @pl.when(comes)
        def _():
            copy.wait_recv()
            acc[j, slot] += in_buf[j, k].astype(jnp.float32)

    def back_after(j, t):
        if t == 0:
            back_start(j, 1, 3)
        elif t == 1:
            back_start(j, 0, 1)
        elif t == 2:
            @pl.when(y == 0)
            def _():
                back_start(j, 2, 4)
        elif t == 3:
            @pl.when(y == 1)
            def _():
                back_add(j, 1, 4)
                back_start(j, 2, 4)

    def back_late(j):
        @pl.when(y == 0)
        def _():
            back_add(j, 1, 2)
        back_add(j, 0, 2 * y)
        back_add(j, 2, 2)
        back_start(j, 3, 2)

    def back_end(j):
        back_add(j, 3, 0)
        cols = slice(j * HEAD_SIZE, (j + 1) * HEAD_SIZE)
        dk_ref[:, cols] = (acc[j, 0, 0] * scale).astype(jnp.bfloat16)
        dv_ref[:, cols] = acc[j, 0, 1].astype(jnp.bfloat16)
        for k in range(4):
            copy, holds, _ = back(j, k)

            @pl.when(holds)
            def _():
                copy.wait_send()

    regroup((0,), 0, start)
    q_in.wait()
    regroup((2, 1), 0, start)
    g_in.wait()
    regroup((3,), 0, start)

    for o in range(1, BLOCKS):
        @pl.when(c < o)
        def _():
            kvb[:, o] = jnp.zeros((kv_count, 2, tokens, HEAD_SIZE), jnp.bfloat16)
    regroup((0,), 0, wait)
    spread(0, 0, 0)

    d_out[...] = jnp.zeros(d_out.shape, jnp.float32)
    o_in.wait()
    l_in.wait()
    ones = jnp.ones((16, HEAD_SIZE), jnp.bfloat16)

    def delta_of(p, carry):
        for i in range(heads):
            cols = pl.ds(pl.multiple_of((p * heads + i) * HEAD_SIZE, HEAD_SIZE), HEAD_SIZE)
            product = g_loc[:, cols].astype(jnp.float32) * o_loc[:, cols].astype(jnp.float32)
            high = product.astype(jnp.bfloat16)
            low = (product - high.astype(jnp.float32)).astype(jnp.bfloat16)
            sums = dot_last(ones, high) + dot_last(ones, low)
            d_out[p, i:i + 1, 0:rows] = sums[0:1]
        return carry

    lax.fori_loop(0, n_head, delta_of, 0)

    def delta_copy(r):
        return pltpu.make_async_remote_copy(
            src_ref=d_out.at[peers[r]], dst_ref=d_in.at[h], send_sem=d_send.at[r], recv_sem=d_recv.at[r],
            device_id=(c, peers[r]), device_id_type=MESH,
        )

    for r in range(n_head - 1):
        delta_copy(r).start()
    d_in[h] = d_out[h]

    spread(0, 0, 1)
    if kv_count > 1:
        regroup((0, 2), 1, start)
    spread(0, 0, 2)
    spread(0, 0, 3)
    for r in range(n_head - 1):
        delta_copy(r).wait()
    for i in range(n_head):
        delta[:, i * rows:(i + 1) * rows] = d_in[i, :, 0:rows]

    bars = []
    for o in range(BLOCKS):
        listed = lists[0, 0] == c - o
        for e in range(1, lists.shape[1]):
            listed = listed | (lists[0, e] == c - o)
        bars.append(jnp.where(listed & (c - o >= 0), 0.0, jnp.inf).astype(jnp.float32))

    def span(w):
        return pl.ds(pl.multiple_of(w * HEAD_SIZE, HEAD_SIZE), HEAD_SIZE)

    def exponentials(j, w):
        q = qb[j, :, span(w)]
        peak = None
        for o in range(BLOCKS):
            s = dot_last(kvb[j, o, 0], q) * (scale * LOG2E)
            sc[w, o] = s
            top = jnp.max(s, axis=0, keepdims=True) - bars[o]
            peak = top if peak is None else jnp.maximum(peak, top)
        total = jnp.zeros_like(peak)
        for o in range(BLOCKS):
            e = jnp.exp2(sc[w, o] - (peak + bars[o]))
            sc[w, o] = e
            total += jnp.sum(e, axis=0, keepdims=True)
        share[pl.ds(w, 1), :] = 1.0 / total
        dq_sum[w] = jnp.zeros(dq_sum.shape[1:], jnp.float32)

    def gradients(j, o):
        value = kvb[j, o, 1]
        key_t = kvb[j, o, 0].T
        dk = dv = None
        for w in range(width):
            cols = slice(w * HEAD_SIZE, (w + 1) * HEAD_SIZE)
            q = qb[j, :, cols]
            g = gb[j, :, cols]
            row = delta[j * width + w:j * width + w + 1, :]
            p = sc[w, o] * share[w:w + 1, :]
            ds = (p * (dot_last(value, g) - row)).astype(jnp.bfloat16)
            dv_term = dot(p.astype(jnp.bfloat16), g)
            dk_term = dot(ds, q)
            dq_sum[w] += dot(key_t, ds)
            dv = dv_term if dv is None else dv + dv_term
            dk = dk_term if dk is None else dk + dk_term
        acc[j, o, 0] = dk
        acc[j, o, 1] = dv

    third = width // 3

    for j in range(kv_count):
        more = j + 1 < kv_count
        regroup((2,), j, wait)
        regroup((1,), j, wait)
        spread(j, 1, 0)

        def first(w, carry):
            for at in (1, 2):
                @pl.when(w == at * third)
                def _():
                    spread(j, 1, at)
                    if j > 0:
                        (back_late, back_end)[at - 1](j - 1)
            exponentials(j, w)
            return carry

        lax.fori_loop(0, width, first, 0)
        spread(j, 1, 3)
        regroup((3,), j, wait)
        if more:
            regroup((1, 3), j + 1, start)
            regroup((0,), j + 1, wait)
            spread(j + 1, 0, 0)

        def second(t, carry):
            gradients(j, lax.rem(3 + 3 * t, BLOCKS))
            for at in range(4):
                @pl.when(t == at)
                def _():
                    back_after(j, at)
                    if more and 1 <= at <= 2:
                        spread(j + 1, 0, at)
            return carry

        lax.fori_loop(0, BLOCKS, second, 0)
        if more:
            spread(j + 1, 0, 3)
        else:
            back_late(j)
        for w in range(width):
            i = j * width + w
            dq_ref[:, i * HEAD_SIZE:(i + 1) * HEAD_SIZE] = (dq_sum[w] * scale).T.astype(jnp.bfloat16)
        if j + 2 < kv_count:
            regroup((0, 2), j + 2, start)
    back_end(kv_count - 1)


def hand_over(*refs):
    sems = refs[-1]
    count = (len(refs) - 1) // 2
    copies = [pltpu.make_async_copy(refs[i], refs[count + i], sems.at[i]) for i in range(count)]
    for copy in copies:
        copy.start()
    for copy in copies:
        copy.wait()


def on_device(n_ctx, n_head, queries, keys, values, outputs, out_grad, frame_lists):
    rows = queries.shape[0]
    tokens = rows * n_head
    kv_count = keys.shape[1] // HEAD_SIZE // n_head
    heads = queries.shape[1] // HEAD_SIZE // n_head
    width = heads // kv_count
    padded = -(-heads // 16) * 16
    assert tokens == FRAME and n_ctx % 2 == 0
    bf, f32 = jnp.bfloat16, jnp.float32
    any_spec = pl.BlockSpec(memory_space=pl.ANY)
    vmem = pl.BlockSpec(memory_space=pltpu.VMEM)
    dma = pltpu.SemaphoreType.DMA
    results = pl.pallas_call(
        functools.partial(kernel, n_ctx, n_head, kv_count, width),
        out_shape=(
            jax.ShapeDtypeStruct((tokens, heads * HEAD_SIZE), bf),
            jax.ShapeDtypeStruct((tokens, kv_count * HEAD_SIZE), bf),
            jax.ShapeDtypeStruct((tokens, kv_count * HEAD_SIZE), bf),
        ),
        in_specs=[any_spec] * 6,
        out_specs=(vmem, vmem, vmem),
        scratch_shapes=[
            pltpu.VMEM((kv_count, tokens, width * HEAD_SIZE), bf),
            pltpu.VMEM((kv_count, tokens, width * HEAD_SIZE), bf),
            pltpu.VMEM((kv_count, BLOCKS, 2, tokens, HEAD_SIZE), bf),
            pltpu.VMEM(queries.shape, bf),
            pltpu.VMEM(out_grad.shape, bf),
            pltpu.VMEM(outputs.shape, bf),
            pltpu.SMEM(frame_lists.shape, jnp.int32),
            pltpu.VMEM((n_head, padded, HEAD_SIZE), f32),
            pltpu.VMEM((n_head, padded, HEAD_SIZE), f32),
            pltpu.VMEM((padded, tokens), f32),
            pltpu.VMEM((width, BLOCKS, tokens, tokens), f32),
            pltpu.VMEM((-(-width // 8) * 8, tokens), f32),
            pltpu.VMEM((width, HEAD_SIZE, tokens), f32),
            pltpu.VMEM((kv_count, BLOCKS, 2, tokens, HEAD_SIZE), f32),
            pltpu.VMEM((kv_count, 4, 2, tokens, HEAD_SIZE), bf),
            pltpu.VMEM((kv_count, 4, 2, tokens, HEAD_SIZE), bf),
            dma((kv_count, 4)),
            dma((4,)),
            dma((n_head - 1, kv_count, 4)),
            dma((n_head - 1, kv_count, 4)),
            dma((n_head - 1,)),
            dma((n_head - 1,)),
            dma((kv_count, 2, 4)),
            dma((kv_count, 2, 4)),
            dma((kv_count, 4)),
            dma((kv_count, 4)),
        ],
        compiler_params=pltpu.CompilerParams(
            collective_id=0, has_side_effects=True, vmem_limit_bytes=60 * 1024 * 1024
        ),
    )(queries, keys, values, outputs, out_grad, frame_lists)
    return pl.pallas_call(
        hand_over,
        out_shape=[jax.ShapeDtypeStruct(x.shape, x.dtype) for x in results],
        in_specs=[any_spec] * 3,
        out_specs=[vmem] * 3,
        scratch_shapes=[dma((3,))],
    )(*results)


def solution(mesh):
    split = P(("ctx", "head"), None)
    return jax.shard_map(
        functools.partial(on_device, mesh.shape["ctx"], mesh.shape["head"]),
        mesh=mesh,
        in_specs=(split,) * 5 + (P("ctx", None),),
        out_specs=(P("ctx", "head"),) * 3,
        check_vma=False,
    )
```
